128 devices in a mesh: gx: 8 (over y, core), gy: 16 (over z, x).
Axes of the slice: x: 4, y: 4, z: 4, core: 2. Of those that a mesh axis runs over, the one named last changes fastest.
Arguments:
- ensemble: float32 [128, 524288], P(('gx', 'gy'))
- obs_owner: int32 [2, 2048], replicated, may hold values from 0 to 127, as said below
- obs_local: int32 [2, 2048], replicated, may hold values from 0 to 4095
- obs_value: float32 [2, 2048], replicated, may hold values from -8 to 8
- obs_errvar: float32 [2, 2048], replicated, may hold values from 0.3 to 3
- tile_list: int32 [2, 2048, 8], replicated, may hold values from -1 to 4095, as said below
- weight_index: int32 [2, 2048, 8], replicated, may hold values from 0 to 15
- weight_table: float32 [16], replicated, may hold values from 0.2 to 1
Outputs:
- analysis: float32 [128, 524288], P(('gx', 'gy'))
The draws below stay inside these ranges and needn't reach their ends.
Inputs may be any that keep to these rules, and one draw needn't show every extreme that they name: `obs_owner`: skewed toward low slabs; the first observation of each batch lies in the last slab, the second in slab 0. `tile_list`: each entry is -1 or a tile within 64 tiles of the observation's own tile, except that the second entry of each batch's first observation is the tile 4096 // 2 tiles away, counted round; tiles may repeat.
All inputs are finite; a program needn't handle non-finite values.
Results may differ from the reference program's by a relative error of at most 0.0003.
Values sent between devices are 32-bit elements; how exact they have to be, the bound alone decides.
No kernel may reach another device: no remote copies, remote signals or barrier semaphores. Data moves between devices by JAX's collectives and lax.ppermute only.
A program may use at most 128 MiB of HBM per device.

```python
import math
import jax
import jax.numpy as jnp
from jax import lax

M = 128
NB = 2
NOB = 2048
KT = 8
NW = 16
TILE = 128
VAR_DEV = 4096
VARS = 524288
NTILES = 4096
DEVICES = 128


def obs_pattern(key):
    keys = jax.random.split(key, 5)
    owners = jnp.minimum(jax.random.randint(keys[0], (NB, NOB), 0, DEVICES), jax.random.randint(keys[1], (NB, NOB), 0, DEVICES))
    owners = owners.at[:, 0].set(DEVICES - 1).at[:, 1].set(0)
    locals_here = jax.random.randint(keys[2], (NB, NOB), 0, VAR_DEV)
    locals_here = locals_here.at[:, 0].set(VAR_DEV - 1).at[:, 1].set(0)
    own_tile = (owners * VAR_DEV + locals_here) // TILE
    reach = 2 * (VAR_DEV // TILE)
    offsets = jax.random.randint(keys[3], (NB, NOB, KT), -reach, reach + 1)
    raw_tiles = own_tile[:, :, None] + offsets
    padded = jax.random.randint(keys[4], (NB, NOB, KT), 0, 4) == 0
    outside = (raw_tiles < 0) | (raw_tiles >= NTILES)
    lists = jnp.where(padded | outside, -1, raw_tiles)
    far_tile = (NTILES - 1 + NTILES // 2) % NTILES
    lists = lists.at[:, 0, 0].set(NTILES - 1).at[:, 0, 1].set(far_tile).at[:, 1, KT - 1].set(-1)
    return (owners.astype(jnp.int32), locals_here.astype(jnp.int32), lists.astype(jnp.int32))


def draw_obs_owner(key, part):
    owners, locals_here, lists = obs_pattern(key)
    return owners


def draw_obs_local(key, part):
    owners, locals_here, lists = obs_pattern(key)
    return locals_here


def draw_tile_list(key, part):
    owners, locals_here, lists = obs_pattern(key)
    return lists


def draw_ensemble(key, part):
    key = jax.random.fold_in(key, 11)
    keys = jax.random.split(key, 4)
    noise = jax.random.normal(keys[0], (M, VARS), jnp.float32)
    scales = jnp.exp(jax.random.uniform(keys[1], (VARS,), jnp.float32, math.log(0.5), math.log(5.0)))
    factor = jax.random.normal(keys[2], (M, NTILES // 2 + 1), jnp.float32)
    tile_of = jnp.arange(VARS, dtype=jnp.int32) // TILE
    shared = factor[:, tile_of // 2] + factor[:, (tile_of + 1) // 2]
    center = jax.random.normal(keys[3], (VARS,), jnp.float32)
    return (center[None, :] + scales[None, :] * (noise + 0.7 * shared)).astype(jnp.float32)


def set_ends(result, own_key, smallest, high):
    extent = result.shape
    place = [jax.random.randint(jax.random.fold_in(own_key, axis), (), 0, extent[axis]) for axis in range(len(extent))]
    result = result.at[tuple(place)].set(smallest)
    longest = extent.index(max(extent))
    place[longest] = (place[longest] + 1) % extent[longest]
    return result.at[tuple(place)].set(high)


def centred(stream_key, shape, scale, most, held_as=jnp.bfloat16):
    entries = scale * jax.random.normal(stream_key, shape, jnp.float32)
    return jnp.clip(entries, min=-most, max=most).astype(held_as)


def setup_inputs(seed: int = 0) -> dict:
    key_list = jax.random.split(jax.random.key(seed), 9)
    return {
        "ensemble": draw_ensemble(jax.random.fold_in(key_list[8], 71), 0),
        "obs_owner": draw_obs_owner(jax.random.fold_in(key_list[8], 71), 0),
        "obs_local": draw_obs_local(jax.random.fold_in(key_list[8], 71), 0),
        "obs_value": centred(key_list[3], (NB, NOB), 1.5, 8.0, jnp.float32),
        "obs_errvar": jnp.clip(jnp.exp(jax.random.uniform(key_list[4], (NB, NOB), jnp.float32, math.log(0.3), math.log(3.0))), 0.3, 3.0),
        "tile_list": draw_tile_list(jax.random.fold_in(key_list[8], 71), 0),
        "weight_index": set_ends(jax.random.randint(key_list[6], (NB, NOB, KT), 0, NW), jax.random.fold_in(key_list[6], 1), 0, NW - 1).astype(jnp.int32),
        "weight_table": jnp.clip(jax.random.uniform(key_list[7], (NW,), jnp.float32, 0.2, 1.0), 0.2, 1.0),
    }


epsilon = 1e-06

def weights_for(tiles_row, index_row, weight_table, first_tile, count):
    tile_ids = first_tile + jnp.arange(count, dtype=jnp.int32)
    tile_hit = (tiles_row[:, :, None] == tile_ids[None, None, :]).astype(jnp.float32)
    table_ids = jnp.arange(weight_table.shape[0], dtype=jnp.int32)
    table_pick = lax.optimization_barrier(jnp.sum((index_row[:, :, None] == table_ids[None, None, :]).astype(jnp.float32) * weight_table[None, None, :], axis=2))
    return lax.optimization_barrier(jnp.sum(tile_hit * table_pick[:, :, None], axis=1))

def increments(priors, value_row, errvar_row):
    members = priors.shape[0]
    obs_mean = lax.optimization_barrier(jnp.mean(priors, axis=0))
    obs_dev = priors - obs_mean
    obs_spread = lax.optimization_barrier(jnp.sum(obs_dev * obs_dev, axis=0)) / (members - 1.0)
    denominator = obs_spread + errvar_row
    post_mean = (errvar_row * obs_mean + obs_spread * value_row) / denominator
    obs_shift = post_mean - obs_mean + (jnp.sqrt(errvar_row / denominator) - 1.0) * obs_dev
    return (obs_dev, obs_spread, obs_shift)

def analyse(slab, obs_dev, obs_spread, obs_shift, weights):
    members, width = slab.shape
    count_obs = obs_dev.shape[1]
    state_mean = lax.optimization_barrier(jnp.mean(slab, axis=0))
    state_dev = slab - state_mean
    covariance = jnp.dot(obs_dev.T, state_dev, precision=lax.Precision.HIGHEST, preferred_element_type=jnp.float32) / (members - 1.0)
    regress = covariance / (obs_spread + epsilon)[:, None]
    localized = (regress.reshape(count_obs, weights.shape[1], width // weights.shape[1]) * weights[:, :, None]).reshape(count_obs, width)
    return slab + jnp.dot(obs_shift, localized, precision=lax.Precision.HIGHEST, preferred_element_type=jnp.float32)

def reference(ensemble, obs_owner, obs_local, obs_value, obs_errvar, tile_list, weight_index, weight_table):
    slab_count = VARS // VAR_DEV
    tiles_slab = VAR_DEV // TILE
    slabs = ensemble
    for batch in range(NB):
        obs_global = obs_owner[batch] * VAR_DEV + obs_local[batch]
        priors = jnp.take(slabs, obs_global, axis=1)
        obs_dev, obs_spread, obs_shift = increments(priors, obs_value[batch], obs_errvar[batch])
        blocks = slabs.reshape(M, slab_count, VAR_DEV).transpose(1, 0, 2)

        def one_slab(pair):
            block, slab_index = pair
            weights = weights_for(tile_list[batch], weight_index[batch], weight_table, slab_index * tiles_slab, tiles_slab)
            return analyse(block, obs_dev, obs_spread, obs_shift, weights)
        updated = lax.map(one_slab, (blocks, jnp.arange(slab_count, dtype=jnp.int32)))
        slabs = updated.transpose(1, 0, 2).reshape(M, VARS)
    return slabs
```

```python
import jax
import jax.numpy as jnp
from jax import lax
from jax.experimental import pallas as pl
from jax.experimental.pallas import tpu as pltpu
from jax.sharding import PartitionSpec as P

TILE = 128
VAR_DEV = 4096
TILES = VAR_DEV // TILE
SLABS = 128
MEMBERS = 128
NOB = 2048
AXES = ("gx", "gy")

SLOTS = 64
FAR_SLOTS = 32
FAR_SLAB = SLABS // 2 - 1
ROWS_OUT = TILES + 8
CHUNK = 256

epsilon = 1e-06
F32 = jnp.float32
BF16 = jnp.bfloat16


def table_lookup(index_row, weight_table):
    table_ids = jnp.arange(weight_table.shape[0], dtype=jnp.int32)
    return jnp.sum(
        (index_row[:, :, None] == table_ids[None, None, :]).astype(jnp.float32)
        * weight_table[None, None, :],
        axis=2,
    )


def weights_for(tiles_row, index_row, weight_table, first_tile, count):
    tile_ids = first_tile + jnp.arange(count, dtype=jnp.int32)
    tile_hit = (tiles_row[:, :, None] == tile_ids[None, None, :]).astype(jnp.float32)
    table_pick = table_lookup(index_row, weight_table)
    return jnp.sum(tile_hit * table_pick[:, :, None], axis=1)


def increments(priors, value_row, errvar_row):
    members = priors.shape[0]
    obs_mean = jnp.mean(priors, axis=0)
    obs_dev = priors - obs_mean
    obs_spread = jnp.sum(obs_dev * obs_dev, axis=0) / (members - 1.0)
    denominator = obs_spread + errvar_row
    post_mean = (errvar_row * obs_mean + obs_spread * value_row) / denominator
    obs_shift = post_mean - obs_mean + (jnp.sqrt(errvar_row / denominator) - 1.0) * obs_dev
    return (obs_dev, obs_spread, obs_shift)


def analyse(slab, obs_dev, obs_spread, obs_shift, weights):
    members, width = slab.shape
    count_obs = obs_dev.shape[1]
    block_obs = min(512, count_obs)
    tiles_here = weights.shape[1]
    state_mean = jnp.mean(slab, axis=0)
    state_dev = slab - state_mean
    total = jnp.zeros_like(slab)
    for start in range(0, count_obs, block_obs):
        dev_part = obs_dev[:, start : start + block_obs]
        covariance = jnp.dot(
            dev_part.T,
            state_dev,
            precision=lax.Precision.HIGHEST,
            preferred_element_type=jnp.float32,
        ) / (members - 1.0)
        regress = covariance / (obs_spread[start : start + block_obs] + epsilon)[:, None]
        localized = (
            regress.reshape(block_obs, tiles_here, width // tiles_here)
            * weights[start : start + block_obs, :, None]
        ).reshape(block_obs, width)
        total = total + jnp.dot(
            obs_shift[:, start : start + block_obs],
            localized,
            precision=lax.Precision.HIGHEST,
            preferred_element_type=jnp.float32,
        )
    return slab + total


def general(ensemble, me, obs_owner, obs_local, obs_value, obs_errvar, tile_list, weight_index, weight_table):
    slabs = lax.all_to_all(ensemble, AXES, split_axis=1, concat_axis=0, tiled=True)
    for batch in range(2):
        owned = (obs_owner[batch] == me).astype(jnp.float32)
        local_rows = jnp.take(slabs, obs_local[batch], axis=1) * owned[None, :]
        mine = lax.all_to_all(local_rows, AXES, split_axis=0, concat_axis=0, tiled=True)
        mine = jnp.broadcast_to(jnp.sum(mine, axis=0), mine.shape)
        priors = lax.all_to_all(mine, AXES, split_axis=0, concat_axis=0, tiled=True)
        obs_dev, obs_spread, obs_shift = increments(priors, obs_value[batch], obs_errvar[batch])
        weights = weights_for(
            tile_list[batch], weight_index[batch], weight_table, me * TILES, TILES
        )
        slabs = analyse(slabs, obs_dev, obs_spread, obs_shift, weights)
    return lax.all_to_all(slabs, AXES, split_axis=0, concat_axis=1, tiled=True)


def dot_nt(a, b):
    return lax.dot_general(a, b, (((1,), (1,)), ((), ())), preferred_element_type=F32)


def dot_tn(a, b):
    return lax.dot_general(a, b, (((0,), (0,)), ((), ())), preferred_element_type=F32)


def dot_nn(a, b):
    return lax.dot_general(a, b, (((1,), (0,)), ((), ())), preferred_element_type=F32)


def split2(x):
    hi = x.astype(BF16)
    return hi, (x - hi.astype(F32)).astype(BF16)


def split3(x):
    hi = x.astype(BF16)
    rest = x - hi.astype(F32)
    mid = rest.astype(BF16)
    return hi, mid, (rest - mid.astype(F32)).astype(BF16)


def iota(shape, axis):
    return lax.broadcasted_iota(jnp.int32, shape, axis)


def send_kernel(tile_s, row_ref, lane_ref, owner_ref, out_ref, key_ref, flag_ref, buf, pad):
    unroll = 16

    def pick(i, carry):
        base = pl.multiple_of(i * unroll, unroll)
        for j in range(unroll):
            buf[pl.ds(base + j, 1), :] = row_ref[pl.ds(tile_s[base + j], 1), :]
        return carry

    lax.fori_loop(0, 2 * NOB // unroll, pick, 0)

    def copy(i, carry):
        src = pl.multiple_of(i * TILES, 8)
        dst = pl.multiple_of(i * ROWS_OUT, 8)
        out_ref[pl.ds(dst, TILES), :] = row_ref[pl.ds(src, TILES), :]
        return carry

    lax.fori_loop(0, SLABS, copy, 0)

    block = 512
    sub128 = iota((128, 128), 0)
    sub = iota((128, block), 0)
    strict = (iota((block, block), 0) < iota((block, block), 1)).astype(F32).astype(BF16)
    ones = jnp.ones((block, 128), BF16)
    pad[...] = jnp.zeros_like(pad)
    over = jnp.zeros((128, 128), F32)
    for b in range(2):
        count = jnp.zeros((128, 128), F32)
        table = jnp.zeros((128, 128), F32)
        for q in range(NOB // block):
            own = owner_ref[b : b + 1, q * block : (q + 1) * block]
            hit = own == sub
            hit16 = hit.astype(F32).astype(BF16)
            before = dot_nn(hit16, strict) + jnp.concatenate([count] * (block // 128), axis=1)
            rank = jnp.sum(jnp.where(hit, before, 0.0), axis=0, keepdims=True).astype(jnp.int32)
            key_ref[b : b + 1, q * block : (q + 1) * block] = own * SLOTS + rank
            slot16 = (rank == (sub & (SLOTS - 1))).astype(F32).astype(BF16)
            pieces = []
            for k in range(block // 128):
                at = b * (NOB // 128) + q * (block // 128) + k
                part = buf[at * 128 : (at + 1) * 128, :].T
                lane = lane_ref[at : at + 1, :]
                pieces.append(jnp.sum(jnp.where(lane == sub128, part, 0.0), axis=0, keepdims=True))
            picked = jnp.concatenate(pieces, axis=1)
            for part in split3(jnp.where(hit, picked, 0.0)):
                table = table + dot_nt(part, slot16)
            count = count + dot_nn(hit16, ones)
        limit = jnp.full((128, 128), float(SLOTS), F32)
        if b == 0:
            limit = jnp.where(sub128 >= SLABS - 3, float(FAR_SLOTS), limit)
        over = jnp.maximum(over, jnp.where(count > limit, 1.0, 0.0))
        pad[b, 8:136, :] = table
    flag_ref[0, 0] = jnp.max(over).astype(jnp.int32)

    low = iota((128, 128), 1) < SLOTS
    for r in range(4):
        out_ref[pl.ds(TILES + r, SLABS, stride=ROWS_OUT), :] = jnp.where(
            low, pad[0, 4 + 2 * r : 132 + 2 * r, :], pad[0, 5 + 2 * r : 133 + 2 * r, :]
        )
    out_ref[pl.ds(TILES + 4, SLABS, stride=ROWS_OUT), :] = jnp.where(
        low, pad[0, 12:140, :], pad[1, 6:134, :]
    )
    for r in range(2):
        out_ref[pl.ds(TILES + 5 + r, SLABS, stride=ROWS_OUT), :] = jnp.where(
            low, pad[1, 7 + 2 * r : 135 + 2 * r, :], pad[1, 8 + 2 * r : 136 + 2 * r, :]
        )
    lanes = iota((1, 128), 1)
    far = jnp.where(
        lanes < 32,
        pad[0, 133:134, :],
        jnp.where(
            lanes < 64,
            pltpu.roll(pad[0, 134:135, :], 32, 1),
            jnp.where(lanes < 96, pad[0, 135:136, :], pltpu.roll(pad[1, 135:136, :], 32, 1)),
        ),
    )
    out_ref[pl.ds(TILES + 7, SLABS, stride=ROWS_OUT), :] = jnp.broadcast_to(far, (128, 128))


def send(ensemble, obs_owner, obs_local):
    tile = (obs_owner * TILES + obs_local // TILE).reshape(2 * NOB)
    lane = (obs_local % TILE).reshape(2 * NOB // 128, 128)
    vmem = pl.BlockSpec(memory_space=pltpu.VMEM)
    smem = pl.BlockSpec(memory_space=pltpu.SMEM)
    return pl.pallas_call(
        send_kernel,
        out_shape=(
            jax.ShapeDtypeStruct((SLABS * ROWS_OUT, 128), F32),
            jax.ShapeDtypeStruct((2, NOB), jnp.int32),
            jax.ShapeDtypeStruct((1, 1), jnp.int32),
        ),
        in_specs=[smem, vmem, vmem, vmem],
        out_specs=(vmem, vmem, smem),
        scratch_shapes=[pltpu.VMEM((2 * NOB, 128), F32), pltpu.VMEM((2, 144, 128), F32)],
        compiler_params=pltpu.CompilerParams(vmem_limit_bytes=40 << 20),
        cost_estimate=pl.CostEstimate(flops=10**9, bytes_accessed=5 << 20, transcendentals=0),
        name="send",
    )(tile, ensemble.reshape(VAR_DEV, 128), lane, obs_owner)


def exact_dot(a, b, dims):
    return lax.dot_general(
        a, b, (dims, ((), ())), precision=lax.Precision.HIGHEST, preferred_element_type=F32
    )


def slot_keys(me):
    def in_range(slab, rank, keep):
        return jnp.where(keep & (slab >= 0) & (slab < SLABS), slab * SLOTS + rank, -1)

    is_far = me == FAR_SLAB
    j = jnp.arange(640, dtype=jnp.int32)
    near0 = in_range(me - 4 + j // SLOTS, j % SLOTS, j < 576)
    f = jnp.arange(128, dtype=jnp.int32)
    reaches_far = jnp.abs(me - FAR_SLAB) <= 2
    far0 = in_range(SLABS - 3 + f // FAR_SLOTS, f % FAR_SLOTS, (f < 96) & reaches_far)
    i = jnp.arange(384, dtype=jnp.int32) - SLOTS
    near1 = in_range(me - 2 + i // SLOTS, i % SLOTS, i >= 0)
    far1 = in_range(jnp.full((128,), SLABS - 1, jnp.int32), f - 96, (f >= 96) & is_far)
    return jnp.concatenate([near0, far0]), jnp.concatenate([near1, far1])


def compaction(weights):
    touch = jnp.any(weights != 0.0, axis=1)
    place = jnp.cumsum(touch.astype(jnp.int32))
    count = place[-1]
    return jnp.where(touch, place - 1, -1), (count + CHUNK - 1) // CHUNK


def tables(me, key, obs_owner, obs_local, obs_value, obs_errvar, tile_list, weight_index, weight_table):
    keys = slot_keys(me)
    cols, rows = [], []
    for b in range(2):
        select = (keys[b][:, None] == key[b][None, :]).astype(F32)
        table_pick = jnp.where(tile_list[b] >= 0, table_lookup(weight_index[b], weight_table), 0.0)
        per_obs = jnp.concatenate([tile_list[b].astype(F32), table_pick], axis=1)
        cols.append(exact_dot(select, per_obs, ((1,), (0,))))
        own_tile = (obs_owner[b] * TILES + obs_local[b] // TILE).astype(F32)
        lines = jnp.stack([obs_value[b], obs_errvar[b], jnp.ones((NOB,), F32), own_tile])
        rows.append(exact_dot(lines, select, ((1,), (1,))))
    near = (me - 2) * TILES + jnp.arange(5 * TILES, dtype=jnp.int32)
    far = jnp.where(me == FAR_SLAB, (SLABS - 1) * TILES + jnp.arange(TILES, dtype=jnp.int32), -2)
    tile_ids = jnp.concatenate([near, far]).astype(F32)

    def on_tiles(col, ids):
        hit = col[:, :8, None] == ids[None, None, :]
        return jnp.sum(jnp.where(hit, col[:, 8:, None], 0.0), axis=1)

    spread0 = on_tiles(cols[0], tile_ids)
    weights0 = spread0[:, 2 * TILES : 3 * TILES]
    weights1 = on_tiles(cols[1], tile_ids[2 * TILES : 3 * TILES])
    meet = (rows[1][3][None, :] == tile_ids[:, None]).astype(F32)
    cross = exact_dot(spread0, meet, ((1,), (0,)))
    place0, chunks0 = compaction(weights0)
    place1, chunks1 = compaction(weights1)
    out = []
    for row, place, weights in ((rows[0], place0, weights0), (rows[1], place1, weights1)):
        occupied = row[2]
        lines = jnp.stack([row[0], row[1] + (1.0 - occupied), place.astype(F32)])
        lines = jnp.concatenate([lines, jnp.zeros((5, lines.shape[1]), F32)])
        out.append((lines, weights.T))
    return jnp.stack([chunks0, chunks1]), cross, out[0], out[1]


def obs_stats(priors, lines):
    value, errvar = lines[0:1, :], lines[1:2, :]
    mean = jnp.mean(priors, axis=0, keepdims=True)
    dev = priors - mean
    spread = jnp.sum(dev * dev, axis=0, keepdims=True) / (MEMBERS - 1.0)
    denominator = spread + errvar
    post_mean = (errvar * mean + spread * value) / denominator
    shift = post_mean - mean + (jnp.sqrt(errvar / denominator) - 1.0) * dev
    scale = 1.0 / ((MEMBERS - 1.0) * (spread + epsilon))
    return dev, shift * scale


def analyse_kernel(
    chunks_s, r_ref, cross_ref, lines0_ref, w0_ref, lines1_ref, w1_ref, out_ref, acc_ref
):
    def payload(r):
        return r_ref[pl.ds(TILES + r, MEMBERS, stride=ROWS_OUT), :]

    def factors(b, dev, gain, lines, w_ref):
        width = dev.shape[1]
        dev_parts = split2(dev)
        gain_parts = split2(gain)
        place = lines[2:3, :].astype(jnp.int32)

        def chunk(c, carry):
            pick = (place == iota((CHUNK, width), 0) + c * CHUNK).astype(F32).astype(BF16)
            dev_hi, dev_lo = [dot_nt(p, pick).astype(BF16) for p in dev_parts]
            gain_c = dot_nt(gain_parts[0], pick) + dot_nt(gain_parts[1], pick)
            dev_both = jnp.concatenate([dev_hi, dev_lo], axis=0)
            w_here = dot_nt(split3(w_ref[...])[0], pick)
            for part in split3(w_ref[...])[1:]:
                w_here = w_here + dot_nt(part, pick)

            for t in range(TILES):
                lhs_hi, lhs_lo = split2(gain_c * w_here[t : t + 1, :])
                both = dot_nt(lhs_hi, dev_both) + dot_nt(lhs_lo, dev_both)
                a = both[:, :128] + both[:, 128:]

                @pl.when(c == 0)
                def _():
                    acc_ref[b, t] = a

                @pl.when(c > 0)
                def _():
                    acc_ref[b, t] = acc_ref[b, t] + a

            return carry

        lax.fori_loop(0, jnp.maximum(chunks_s[b], 1), chunk, 0)

    part_rows = [payload(r) for r in range(8)]
    priors0 = jnp.concatenate([part_rows[r] for r in (0, 1, 2, 3, 4, 7)], axis=1)
    priors1 = jnp.concatenate([part_rows[r] for r in (4, 5, 6, 7)], axis=1)
    dev0, gain0 = obs_stats(priors0, lines0_ref)

    dev_hi, dev_lo = split2(dev0)
    z_dev = priors1 - jnp.mean(priors1, axis=0, keepdims=True)
    z_hi, z_lo = split2(z_dev)
    covariance = dot_tn(
        jnp.concatenate([dev_hi, dev_lo], axis=0), jnp.concatenate([z_hi, z_hi], axis=0)
    ) + dot_tn(dev_hi, z_lo)
    c_hi, c_lo = split2(covariance * cross_ref[...])
    g_hi, g_lo = split2(gain0)
    priors1 = priors1 + (dot_nn(g_hi, c_hi) + dot_nn(g_lo, c_hi) + dot_nn(g_hi, c_lo))
    dev1, gain1 = obs_stats(priors1, lines1_ref)

    factors(0, dev0, gain0, lines0_ref, w0_ref)
    factors(1, dev1, gain1, lines1_ref, w1_ref)

    def update(b, t, x):
        dev = x - jnp.mean(x, axis=0, keepdims=True)
        hi, lo = split2(dev)
        both = jnp.concatenate([hi, lo], axis=1)
        a_hi, a_lo = split2(acc_ref[b, t])
        step = dot_nn(jnp.concatenate([a_hi, a_lo], axis=1), jnp.concatenate([both, both], axis=0))
        return x + (step[:, :128] + step[:, 128:])

    for t in range(TILES):
        x = r_ref[pl.ds(t, MEMBERS, stride=ROWS_OUT), :]
        x = update(0, t, x)
        x = update(1, t, x)
        out_ref[pl.ds(t, MEMBERS, stride=TILES), :] = x


def analyse_slab(received, chunks, cross, obs0, obs1):
    vmem = pl.BlockSpec(memory_space=pltpu.VMEM)
    smem = pl.BlockSpec(memory_space=pltpu.SMEM)
    return pl.pallas_call(
        analyse_kernel,
        out_shape=jax.ShapeDtypeStruct((MEMBERS * TILES, 128), F32),
        in_specs=[smem] + [vmem] * 6,
        out_specs=vmem,
        scratch_shapes=[pltpu.VMEM((2, TILES, MEMBERS, MEMBERS), F32)],
        compiler_params=pltpu.CompilerParams(vmem_limit_bytes=48 << 20),
        cost_estimate=pl.CostEstimate(flops=4 * 10**9, bytes_accessed=8 << 20, transcendentals=0),
        name="analyse",
    )(chunks, received, cross, obs0[0], obs0[1], obs1[0], obs1[1])


def body(
    ensemble, obs_owner, obs_local, obs_value, obs_errvar, tile_list, weight_index, weight_table
):
    me = lax.axis_index("gx") * lax.axis_size("gy") + lax.axis_index("gy")
    obs = (obs_owner, obs_local, obs_value, obs_errvar, tile_list, weight_index, weight_table)
    outgoing, key, flag = send(ensemble, obs_owner, obs_local)

    received = lax.all_to_all(
        outgoing.reshape(SLABS, ROWS_OUT, 128), AXES, split_axis=0, concat_axis=0, tiled=True
    ).reshape(MEMBERS * ROWS_OUT, 128)
    chunks, cross, obs0, obs1 = tables(me, key, *obs)
    updated = analyse_slab(received, chunks, cross, obs0, obs1)
    result = lax.all_to_all(
        updated.reshape(MEMBERS, TILES, 128), AXES, split_axis=0, concat_axis=0, tiled=True
    ).reshape(ensemble.shape)

    def overflows(state):
        return state[0] > 0

    def redo(state):
        return jnp.int32(0), general(ensemble, me, *obs)

    return lax.while_loop(overflows, redo, (flag[0, 0], result))[1]


def solution(mesh):
    placed = (P(("gx", "gy"), None), P(), P(), P(), P(), P(), P(), P())
    return jax.shard_map(
        body, mesh=mesh, in_specs=placed, out_specs=P(("gx", "gy"), None), check_vma=False
    )
```

```python
import jax
import jax.numpy as jnp
from jax import lax
from jax.experimental import pallas as pl
from jax.experimental.pallas import tpu as pltpu
from jax.sharding import PartitionSpec as P

TILE = 128
VAR_DEV = 4096
TILES = VAR_DEV // TILE
SLABS = 128
MEMBERS = 128
NOB = 2048
AXES = ("gx", "gy")

SLOTS = 64
FAR_SLOTS = 32
FAR_SLAB = SLABS // 2 - 1
ROWS_OUT = TILES + 8
CHUNK = 256
GROUP = 4

epsilon = 1e-06
F32 = jnp.float32
BF16 = jnp.bfloat16


def table_lookup(index_row, weight_table):
    table_ids = jnp.arange(weight_table.shape[0], dtype=jnp.int32)
    return jnp.sum(
        (index_row[:, :, None] == table_ids[None, None, :]).astype(jnp.float32)
        * weight_table[None, None, :],
        axis=2,
    )


def weights_for(tiles_row, index_row, weight_table, first_tile, count):
    tile_ids = first_tile + jnp.arange(count, dtype=jnp.int32)
    tile_hit = (tiles_row[:, :, None] == tile_ids[None, None, :]).astype(jnp.float32)
    table_pick = table_lookup(index_row, weight_table)
    return jnp.sum(tile_hit * table_pick[:, :, None], axis=1)


def increments(priors, value_row, errvar_row):
    members = priors.shape[0]
    obs_mean = jnp.mean(priors, axis=0)
    obs_dev = priors - obs_mean
    obs_spread = jnp.sum(obs_dev * obs_dev, axis=0) / (members - 1.0)
    denominator = obs_spread + errvar_row
    post_mean = (errvar_row * obs_mean + obs_spread * value_row) / denominator
    obs_shift = post_mean - obs_mean + (jnp.sqrt(errvar_row / denominator) - 1.0) * obs_dev
    return (obs_dev, obs_spread, obs_shift)


def analyse(slab, obs_dev, obs_spread, obs_shift, weights):
    members, width = slab.shape
    count_obs = obs_dev.shape[1]
    block_obs = min(512, count_obs)
    tiles_here = weights.shape[1]
    state_mean = jnp.mean(slab, axis=0)
    state_dev = slab - state_mean
    total = jnp.zeros_like(slab)
    for start in range(0, count_obs, block_obs):
        dev_part = obs_dev[:, start : start + block_obs]
        covariance = jnp.dot(
            dev_part.T,
            state_dev,
            precision=lax.Precision.HIGHEST,
            preferred_element_type=jnp.float32,
        ) / (members - 1.0)
        regress = covariance / (obs_spread[start : start + block_obs] + epsilon)[:, None]
        localized = (
            regress.reshape(block_obs, tiles_here, width // tiles_here)
            * weights[start : start + block_obs, :, None]
        ).reshape(block_obs, width)
        total = total + jnp.dot(
            obs_shift[:, start : start + block_obs],
            localized,
            precision=lax.Precision.HIGHEST,
            preferred_element_type=jnp.float32,
        )
    return slab + total


def general(slabs, me, obs_owner, obs_local, obs_value, obs_errvar, tile_list, weight_index, weight_table):
    for batch in range(2):
        owned = (obs_owner[batch] == me).astype(jnp.float32)
        local_rows = jnp.take(slabs, obs_local[batch], axis=1) * owned[None, :]
        mine = lax.all_to_all(local_rows, AXES, split_axis=0, concat_axis=0, tiled=True)
        mine = jnp.broadcast_to(jnp.sum(mine, axis=0), mine.shape)
        priors = lax.all_to_all(mine, AXES, split_axis=0, concat_axis=0, tiled=True)
        obs_dev, obs_spread, obs_shift = increments(priors, obs_value[batch], obs_errvar[batch])
        weights = weights_for(
            tile_list[batch], weight_index[batch], weight_table, me * TILES, TILES
        )
        slabs = analyse(slabs, obs_dev, obs_spread, obs_shift, weights)
    return slabs


def dot_nt(a, b):
    return lax.dot_general(a, b, (((1,), (1,)), ((), ())), preferred_element_type=F32)


def dot_tn(a, b):
    return lax.dot_general(a, b, (((0,), (0,)), ((), ())), preferred_element_type=F32)


def dot_nn(a, b):
    return lax.dot_general(a, b, (((1,), (0,)), ((), ())), preferred_element_type=F32)


def split2(x):
    hi = x.astype(BF16)
    return hi, (x - hi.astype(F32)).astype(BF16)


def split3(x):
    hi = x.astype(BF16)
    rest = x - hi.astype(F32)
    mid = rest.astype(BF16)
    return hi, mid, (rest - mid.astype(F32)).astype(BF16)


def iota(shape, axis):
    return lax.broadcasted_iota(jnp.int32, shape, axis)


def send_kernel(
    x_ref, owner_ref, local_ref, out_ref, key_ref, flag_ref, row, buf, pad, pay, tile_v, tile_s0, tile_s1, sems
):
    unroll = 64
    block = 512
    lane_bits = TILE - 1
    load = pltpu.make_async_copy(x_ref, row, sems.at[0])
    load.start()
    tile_v[...] = owner_ref[...] * TILES + lax.shift_right_logical(local_ref[...], 7)
    index0 = pltpu.make_async_copy(tile_v.at[0], tile_s0, sems.at[1])
    index1 = pltpu.make_async_copy(tile_v.at[1], tile_s1, sems.at[4])
    index0.start()
    index1.start()

    sub128 = iota((128, 128), 0)
    sub = iota((128, block), 0)
    strict = (iota((block, block), 0) < iota((block, block), 1)).astype(F32).astype(BF16)
    ones = jnp.ones((block, 128), BF16)
    pad[...] = jnp.zeros_like(pad)
    over = jnp.zeros((128, 128), F32)
    ranks = []
    for b in range(2):
        count = jnp.zeros((128, 128), F32)
        for q in range(NOB // block):
            own = owner_ref[b : b + 1, q * block : (q + 1) * block]
            hit = own == sub
            hit16 = hit.astype(F32).astype(BF16)
            before = dot_nn(hit16, strict) + jnp.concatenate([count] * (block // 128), axis=1)
            rank = jnp.sum(jnp.where(hit, before, 0.0), axis=0, keepdims=True).astype(jnp.int32)
            key_ref[b : b + 1, q * block : (q + 1) * block] = own * SLOTS + rank
            ranks.append(rank)
            count = count + dot_nn(hit16, ones)
        limit = jnp.full((128, 128), float(SLOTS), F32)
        if b == 0:
            limit = jnp.where(sub128 >= SLABS - 3, float(FAR_SLOTS), limit)
        over = jnp.maximum(over, jnp.where(count > limit, 1.0, 0.0))
    flag_ref[0, 0] = jnp.max(over).astype(jnp.int32)

    index0.wait()
    index1.wait()
    load.wait()
    slab = pltpu.make_async_copy(
        row.reshape(SLABS, TILES, 128), out_ref.at[:, 0:TILES, :], sems.at[2]
    )
    slab.start()

    for b, tile_s in enumerate((tile_s0, tile_s1)):

        def pick(i, carry, b=b, tile_s=tile_s):
            base = pl.multiple_of(i * unroll, unroll)
            for j in range(unroll):
                buf[pl.ds(b * NOB + base + j, 1), :] = row[pl.ds(tile_s[base + j], 1), :]
            return carry

        lax.fori_loop(0, NOB // unroll, pick, 0)

    for b in range(2):
        table = jnp.zeros((128, 128), F32)
        for q in range(NOB // block):
            own = owner_ref[b : b + 1, q * block : (q + 1) * block]
            hit = own == sub
            slot16 = (ranks[b * (NOB // block) + q] == (sub & (SLOTS - 1))).astype(F32).astype(BF16)
            pieces = []
            for k in range(block // 128):
                at = q * block + k * 128
                part = buf[b * NOB + at : b * NOB + at + 128, :].T
                lane = local_ref[b : b + 1, at : at + 128] & lane_bits
                pieces.append(jnp.sum(jnp.where(lane == sub128, part, 0.0), axis=0, keepdims=True))
            picked = jnp.concatenate(pieces, axis=1)
            for part in split3(jnp.where(hit, picked, 0.0)):
                table = table + dot_nt(part, slot16)
        pad[b, 8:136, :] = table

    low = iota((128, 128), 1) < SLOTS
    for r in range(4):
        pay[:, r, :] = jnp.where(
            low, pad[0, 4 + 2 * r : 132 + 2 * r, :], pad[0, 5 + 2 * r : 133 + 2 * r, :]
        )
    pay[:, 4, :] = jnp.where(low, pad[0, 12:140, :], pad[1, 6:134, :])
    for r in range(2):
        pay[:, 5 + r, :] = jnp.where(
            low, pad[1, 7 + 2 * r : 135 + 2 * r, :], pad[1, 8 + 2 * r : 136 + 2 * r, :]
        )
    lanes = iota((1, 128), 1)
    far = jnp.where(
        lanes < 32,
        pad[0, 133:134, :],
        jnp.where(
            lanes < 64,
            pltpu.roll(pad[0, 134:135, :], 32, 1),
            jnp.where(lanes < 96, pad[0, 135:136, :], pltpu.roll(pad[1, 135:136, :], 32, 1)),
        ),
    )
    pay[:, 7, :] = jnp.broadcast_to(far, (128, 128))
    window = pltpu.make_async_copy(pay, out_ref.at[:, TILES:ROWS_OUT, :], sems.at[3])
    window.start()
    slab.wait()
    window.wait()


def send(ensemble, obs_owner, obs_local):
    vmem = pl.BlockSpec(memory_space=pltpu.VMEM)
    smem = pl.BlockSpec(memory_space=pltpu.SMEM)
    hbm = pl.BlockSpec(memory_space=pl.ANY)
    return pl.pallas_call(
        send_kernel,
        out_shape=(
            jax.ShapeDtypeStruct((SLABS, ROWS_OUT, 128), F32),
            jax.ShapeDtypeStruct((2, NOB), jnp.int32),
            jax.ShapeDtypeStruct((1, 1), jnp.int32),
        ),
        in_specs=[hbm, vmem, vmem],
        out_specs=(hbm, vmem, smem),
        scratch_shapes=[
            pltpu.VMEM((VAR_DEV, 128), F32),
            pltpu.VMEM((2 * NOB, 128), F32),
            pltpu.VMEM((2, 144, 128), F32),
            pltpu.VMEM((SLABS, 8, 128), F32),
            pltpu.VMEM((2, NOB), jnp.int32),
            pltpu.SMEM((NOB,), jnp.int32),
            pltpu.SMEM((NOB,), jnp.int32),
            pltpu.SemaphoreType.DMA((5,)),
        ],
        compiler_params=pltpu.CompilerParams(vmem_limit_bytes=60 << 20),
        cost_estimate=pl.CostEstimate(flops=10**9, bytes_accessed=5 << 20, transcendentals=0),
        name="send",
    )(ensemble.reshape(VAR_DEV, 128), obs_owner, obs_local)


SLOTS0 = 768
SLOTS1 = 512
CROSS_TILES = 256


def tables_kernel(
    me_s,
    table_s,
    key_ref,
    owner_ref,
    local_ref,
    value_ref,
    errvar_ref,
    list_ref,
    index_ref,
    cross_ref,
    lines0_ref,
    w0_ref,
    lines1_ref,
    w1_ref,
    chunks_ref,
):
    me = me_s[0, 0]
    at_far = me == FAR_SLAB
    near_far = (me >= FAR_SLAB - 2) & (me <= FAR_SLAB + 2)

    def slot_key(slab, rank, keep):
        return jnp.where(keep & (slab >= 0) & (slab < SLABS), slab * SLOTS + rank, -1)

    j = iota((SLOTS0, 128), 0)
    f = j - 640
    near = slot_key(me - 4 + lax.shift_right_logical(j, 6), j & 63, j < 576)
    far = slot_key(SLABS - 3 + lax.shift_right_arithmetic(f, 5), f & 31, (f < 96) & near_far)
    keys0 = jnp.where(j < 640, near, far)
    j = iota((SLOTS1, 128), 0)
    f = j - 384
    near = slot_key(me - 3 + lax.shift_right_logical(j, 6), j & 63, j >= 64)
    far = slot_key(jnp.full_like(j, SLABS - 1), f - 96, (f >= 96) & at_far)
    keys1 = jnp.where(j < 384, near, far)

    def tile_id(shape):
        k = iota(shape, 0)
        near_id = (me - 2) * TILES + k
        far_id = jnp.where((k < 192) & at_far, (SLABS - 1) * TILES + k - 160, -2)
        return jnp.where(k < 160, jnp.where(near_id < 0, -2, near_id), far_id)

    def on_tiles(b, ids):
        total = jnp.zeros(ids.shape, F32)
        for k in range(8):
            entry = index_ref[b, k : k + 1, :]
            pick = jnp.zeros(entry.shape, F32)
            for n in range(16):
                pick = jnp.where(entry == n, table_s[n], pick)
            total = total + jnp.where(list_ref[b, k : k + 1, :] == ids, pick, 0.0)
        return total

    def exact_nt(a, b):
        return sum(dot_nt(part, b) for part in split3(a))

    ids = tile_id((CROSS_TILES, NOB))
    own_ids = me * TILES + iota((TILES, NOB), 0)
    for b, (keys, lines_ref, w_ref) in enumerate(
        ((keys0, lines0_ref, w0_ref), (keys1, lines1_ref, w1_ref))
    ):
        slots = keys.shape[0]
        select = jnp.concatenate(
            [
                (keys == key_ref[b : b + 1, c * 128 : (c + 1) * 128]).astype(F32).astype(BF16)
                for c in range(NOB // 128)
            ],
            axis=1,
        )
        own_tile = owner_ref[b : b + 1, :] * TILES + lax.shift_right_logical(local_ref[b : b + 1, :], 7)
        lines = jnp.concatenate(
            [
                value_ref[b : b + 1, :],
                errvar_ref[b : b + 1, :] - 1.0,
                own_tile.astype(F32) + 1.0,
                jnp.zeros((5, NOB), F32),
            ],
            axis=0,
        )
        lines = exact_nt(lines, select)
        weights = exact_nt(on_tiles(b, own_ids), select)
        touch = jnp.max(jnp.where(weights != 0.0, 1.0, 0.0), axis=0, keepdims=True)
        upto = (iota((slots, slots), 0) <= iota((slots, slots), 1)).astype(F32).astype(BF16)
        place = dot_nn(jnp.broadcast_to(touch, (8, slots)).astype(BF16), upto)[0:1, :]
        chunks_ref[b] = (jnp.max(place).astype(jnp.int32) + CHUNK - 1) // CHUNK
        w_ref[...] = weights
        lines_ref[...] = jnp.concatenate(
            [
                lines[0:1, :],
                lines[1:2, :] + 1.0,
                jnp.where(touch > 0.0, place - 1.0, -1.0),
                jnp.zeros((5, slots), F32),
            ],
            axis=0,
        )
        if b == 0:
            spread = on_tiles(0, ids)
            spread = [dot_nt(select, part).astype(BF16) for part in split3(spread)]
        else:
            own_row = lines[2:3, :].astype(jnp.int32) - 1
            meet = (own_row == tile_id((CROSS_TILES, slots))).astype(F32).astype(BF16)
            cross_ref[...] = sum(dot_nn(part, meet) for part in spread)


def tables(me, key, obs_owner, obs_local, obs_value, obs_errvar, tile_list, weight_index, weight_table):
    vmem = pl.BlockSpec(memory_space=pltpu.VMEM)
    smem = pl.BlockSpec(memory_space=pltpu.SMEM)
    cross, lines0, w0, lines1, w1, chunks = pl.pallas_call(
        tables_kernel,
        out_shape=(
            jax.ShapeDtypeStruct((SLOTS0, SLOTS1), F32),
            jax.ShapeDtypeStruct((8, SLOTS0), F32),
            jax.ShapeDtypeStruct((TILES, SLOTS0), F32),
            jax.ShapeDtypeStruct((8, SLOTS1), F32),
            jax.ShapeDtypeStruct((TILES, SLOTS1), F32),
            jax.ShapeDtypeStruct((2,), jnp.int32),
        ),
        in_specs=[smem, smem] + [vmem] * 7,
        out_specs=(vmem, vmem, vmem, vmem, vmem, smem),
        compiler_params=pltpu.CompilerParams(vmem_limit_bytes=28 << 20),
        cost_estimate=pl.CostEstimate(flops=10**6, bytes_accessed=10**6, transcendentals=0),
        name="tables",
    )(
        me.reshape(1, 1).astype(jnp.int32),
        weight_table,
        key,
        obs_owner,
        obs_local,
        obs_value,
        obs_errvar,
        jnp.transpose(tile_list, (0, 2, 1)),
        jnp.transpose(weight_index, (0, 2, 1)),
    )
    return chunks, cross, (lines0, w0), (lines1, w1)


def obs_stats(priors, lines):
    value, errvar = lines[0:1, :], lines[1:2, :]
    mean = jnp.mean(priors, axis=0, keepdims=True)
    dev = priors - mean
    spread = jnp.sum(dev * dev, axis=0, keepdims=True) / (MEMBERS - 1.0)
    denominator = spread + errvar
    post_mean = (errvar * mean + spread * value) / denominator
    shift = post_mean - mean + (jnp.sqrt(errvar / denominator) - 1.0) * dev
    scale = 1.0 / ((MEMBERS - 1.0) * (spread + epsilon))
    return dev, shift * scale


def analyse_kernel(
    chunks_s, r_ref, cross_ref, lines0_ref, w0_ref, lines1_ref, w1_ref, out_ref, acc_ref, x_ref, sems
):
    received = r_ref.reshape(MEMBERS * ROWS_OUT, 128)

    def tile(t):
        return received[pl.ds(t, MEMBERS, stride=ROWS_OUT), :]

    def payload(r):
        return tile(TILES + r)

    def pick_of(place, c):
        return (place == iota((CHUNK, place.shape[1]), 0) + c * CHUNK).astype(F32).astype(BF16)

    def weights_of(w_ref, pick):
        return sum(dot_nt(part, pick) for part in split3(w_ref[...]))

    early = []
    for lines_ref, w_ref in ((lines0_ref, w0_ref), (lines1_ref, w1_ref)):
        pick = pick_of(lines_ref[2:3, :].astype(jnp.int32), 0)
        early.append((pick, weights_of(w_ref, pick)))

    def factors(b, dev, gain, lines, w_ref):
        width = dev.shape[1]
        dev_parts = split2(dev)
        gain_parts = split2(gain)
        place = lines[2:3, :].astype(jnp.int32)

        def chunk(c, first):
            if first:
                pick, w_here = early[b]
            else:
                pick = pick_of(place, c)
                w_here = weights_of(w_ref, pick)
            dev_both = jnp.concatenate([dot_nt(pick, p).astype(BF16) for p in dev_parts], axis=1)
            gain_c = dot_nt(gain_parts[0], pick) + dot_nt(gain_parts[1], pick)
            for start in range(0, TILES, GROUP):
                lhs = []
                for t in range(start, start + GROUP):
                    lhs.extend(split2(gain_c * w_here[t : t + 1, :]))
                both = dot_nn(jnp.concatenate(lhs, axis=0), dev_both)
                both = both[:, :128] + both[:, 128:]
                for k in range(GROUP):
                    a = both[256 * k : 256 * k + 128, :] + both[256 * k + 128 : 256 * k + 256, :]
                    acc_ref[b, start + k] = a if first else acc_ref[b, start + k] + a

        def more(c, carry):
            chunk(c, False)
            return carry

        chunk(0, True)
        lax.fori_loop(1, chunks_s[b], more, 0)

    part_rows = [payload(r) for r in range(8)]
    priors0 = jnp.concatenate([part_rows[r] for r in (0, 1, 2, 3, 4, 7)], axis=1)
    priors1 = jnp.concatenate([part_rows[r] for r in (4, 5, 6, 7)], axis=1)
    dev0, gain0 = obs_stats(priors0, lines0_ref)

    dev_hi, dev_lo = split2(dev0)
    z_dev = priors1 - jnp.mean(priors1, axis=0, keepdims=True)
    z_hi, z_lo = split2(z_dev)
    covariance = dot_tn(
        jnp.concatenate([dev_hi, dev_lo], axis=0), jnp.concatenate([z_hi, z_hi], axis=0)
    ) + dot_tn(dev_hi, z_lo)
    c_hi, c_lo = split2(covariance * cross_ref[...])
    g_hi, g_lo = split2(gain0)
    priors1 = priors1 + (dot_nn(g_hi, c_hi) + dot_nn(g_lo, c_hi) + dot_nn(g_hi, c_lo))
    dev1, gain1 = obs_stats(priors1, lines1_ref)

    factors(0, dev0, gain0, lines0_ref, w0_ref)
    factors(1, dev1, gain1, lines1_ref, w1_ref)

    def update(b, t, x):
        dev = x - jnp.mean(x, axis=0, keepdims=True)
        hi, lo = split2(dev)
        both = jnp.concatenate([hi, lo], axis=1)
        a_hi, a_lo = split2(acc_ref[b, t])
        step = dot_nn(jnp.concatenate([a_hi, a_lo], axis=1), jnp.concatenate([both, both], axis=0))
        return x + (step[:, :128] + step[:, 128:])

    leave = []
    for start in range(0, TILES, 8):
        group = range(start, start + 8)
        for t in group:
            x_ref[t] = update(1, t, update(0, t, tile(t)))
        for t in group:
            copy = pltpu.make_async_copy(x_ref.at[t], out_ref.at[:, t, :], sems.at[t])
            copy.start()
            leave.append(copy)
    for copy in leave:
        copy.wait()


def analyse_slab(received, chunks, cross, obs0, obs1):
    vmem = pl.BlockSpec(memory_space=pltpu.VMEM)
    smem = pl.BlockSpec(memory_space=pltpu.SMEM)
    hbm = pl.BlockSpec(memory_space=pl.ANY)
    return pl.pallas_call(
        analyse_kernel,
        out_shape=jax.ShapeDtypeStruct((MEMBERS, TILES, 128), F32),
        in_specs=[smem] + [vmem] * 6,
        out_specs=hbm,
        scratch_shapes=[
            pltpu.VMEM((2, TILES, MEMBERS, MEMBERS), F32),
            pltpu.VMEM((TILES, MEMBERS, 128), F32),
            pltpu.SemaphoreType.DMA((TILES,)),
        ],
        compiler_params=pltpu.CompilerParams(vmem_limit_bytes=24 << 20),
        cost_estimate=pl.CostEstimate(flops=4 * 10**9, bytes_accessed=8 << 20, transcendentals=0),
        name="analyse",
    )(chunks, received, cross, obs0[0], obs0[1], obs1[0], obs1[1])


def body(
    ensemble, obs_owner, obs_local, obs_value, obs_errvar, tile_list, weight_index, weight_table
):
    me = lax.axis_index("gx") * lax.axis_size("gy") + lax.axis_index("gy")
    obs = (obs_owner, obs_local, obs_value, obs_errvar, tile_list, weight_index, weight_table)
    outgoing, key, flag = send(ensemble, obs_owner, obs_local)

    received = lax.all_to_all(outgoing, AXES, split_axis=0, concat_axis=0, tiled=True)
    chunks, cross, obs0, obs1 = tables(me, key, *obs)
    updated = analyse_slab(received, chunks, cross, obs0, obs1)

    def overflows(state):
        return state[0] > 0

    def redo(state):
        slabs = received[:, :TILES, :].reshape(MEMBERS, VAR_DEV)
        return jnp.int32(0), general(slabs, me, *obs).reshape(MEMBERS, TILES, 128)

    updated = lax.while_loop(overflows, redo, (flag[0, 0], updated))[1]
    result = lax.all_to_all(updated, AXES, split_axis=0, concat_axis=0, tiled=True)
    return result.reshape(ensemble.shape)


def solution(mesh):
    placed = (P(("gx", "gy"), None), P(), P(), P(), P(), P(), P(), P())
    return jax.shard_map(
        body, mesh=mesh, in_specs=placed, out_specs=P(("gx", "gy"), None), check_vma=False
    )
```

```python
import jax
import jax.numpy as jnp
from jax import lax
from jax.experimental import pallas as pl
from jax.experimental.pallas import tpu as pltpu
from jax.sharding import PartitionSpec as P

TILE = 128
VAR_DEV = 4096
TILES = VAR_DEV // TILE
SLABS = 128
MEMBERS = 128
NOB = 2048
AXES = ("gx", "gy")

SLOTS = 64
FAR_SLOTS = 32
FAR_SLAB = SLABS // 2 - 1
ROWS_OUT = TILES + 8
PER_TILE = 32
GROUP = 16

epsilon = 1e-06
F32 = jnp.float32
BF16 = jnp.bfloat16


def table_lookup(index_row, weight_table):
    table_ids = jnp.arange(weight_table.shape[0], dtype=jnp.int32)
    return jnp.sum(
        (index_row[:, :, None] == table_ids[None, None, :]).astype(jnp.float32)
        * weight_table[None, None, :],
        axis=2,
    )


def weights_for(tiles_row, index_row, weight_table, first_tile, count):
    tile_ids = first_tile + jnp.arange(count, dtype=jnp.int32)
    tile_hit = (tiles_row[:, :, None] == tile_ids[None, None, :]).astype(jnp.float32)
    table_pick = table_lookup(index_row, weight_table)
    return jnp.sum(tile_hit * table_pick[:, :, None], axis=1)


def increments(priors, value_row, errvar_row):
    members = priors.shape[0]
    obs_mean = jnp.mean(priors, axis=0)
    obs_dev = priors - obs_mean
    obs_spread = jnp.sum(obs_dev * obs_dev, axis=0) / (members - 1.0)
    denominator = obs_spread + errvar_row
    post_mean = (errvar_row * obs_mean + obs_spread * value_row) / denominator
    obs_shift = post_mean - obs_mean + (jnp.sqrt(errvar_row / denominator) - 1.0) * obs_dev
    return (obs_dev, obs_spread, obs_shift)


def analyse(slab, obs_dev, obs_spread, obs_shift, weights):
    members, width = slab.shape
    count_obs = obs_dev.shape[1]
    block_obs = min(512, count_obs)
    tiles_here = weights.shape[1]
    state_mean = jnp.mean(slab, axis=0)
    state_dev = slab - state_mean
    total = jnp.zeros_like(slab)
    for start in range(0, count_obs, block_obs):
        dev_part = obs_dev[:, start : start + block_obs]
        covariance = jnp.dot(
            dev_part.T,
            state_dev,
            precision=lax.Precision.HIGHEST,
            preferred_element_type=jnp.float32,
        ) / (members - 1.0)
        regress = covariance / (obs_spread[start : start + block_obs] + epsilon)[:, None]
        localized = (
            regress.reshape(block_obs, tiles_here, width // tiles_here)
            * weights[start : start + block_obs, :, None]
        ).reshape(block_obs, width)
        total = total + jnp.dot(
            obs_shift[:, start : start + block_obs],
            localized,
            precision=lax.Precision.HIGHEST,
            preferred_element_type=jnp.float32,
        )
    return slab + total


def general(slabs, me, obs_owner, obs_local, obs_value, obs_errvar, tile_list, weight_index, weight_table):
    for batch in range(2):
        owned = (obs_owner[batch] == me).astype(jnp.float32)
        local_rows = jnp.take(slabs, obs_local[batch], axis=1) * owned[None, :]
        mine = lax.all_to_all(local_rows, AXES, split_axis=0, concat_axis=0, tiled=True)
        mine = jnp.broadcast_to(jnp.sum(mine, axis=0), mine.shape)
        priors = lax.all_to_all(mine, AXES, split_axis=0, concat_axis=0, tiled=True)
        obs_dev, obs_spread, obs_shift = increments(priors, obs_value[batch], obs_errvar[batch])
        weights = weights_for(
            tile_list[batch], weight_index[batch], weight_table, me * TILES, TILES
        )
        slabs = analyse(slabs, obs_dev, obs_spread, obs_shift, weights)
    return slabs


def dot_nt(a, b):
    return lax.dot_general(a, b, (((1,), (1,)), ((), ())), preferred_element_type=F32)


def dot_tn(a, b):
    return lax.dot_general(a, b, (((0,), (0,)), ((), ())), preferred_element_type=F32)


def dot_nn(a, b):
    return lax.dot_general(a, b, (((1,), (0,)), ((), ())), preferred_element_type=F32)


def split2(x):
    hi = x.astype(BF16)
    return hi, (x - hi.astype(F32)).astype(BF16)


def split3(x):
    hi = x.astype(BF16)
    rest = x - hi.astype(F32)
    mid = rest.astype(BF16)
    return hi, mid, (rest - mid.astype(F32)).astype(BF16)


def iota(shape, axis):
    return lax.broadcasted_iota(jnp.int32, shape, axis)


def send_kernel(
    x_ref, owner_ref, local_ref, out_ref, key_ref, flag_ref, row, buf, pad, pay, tile_v, tile_s0, tile_s1, sems
):
    unroll = 64
    block = 512
    lane_bits = TILE - 1
    load = pltpu.make_async_copy(x_ref, row, sems.at[0])
    load.start()
    tile_v[...] = owner_ref[...] * TILES + lax.shift_right_logical(local_ref[...], 7)
    index0 = pltpu.make_async_copy(tile_v.at[0], tile_s0, sems.at[1])
    index1 = pltpu.make_async_copy(tile_v.at[1], tile_s1, sems.at[4])
    index0.start()
    index1.start()

    sub128 = iota((128, 128), 0)
    sub = iota((128, block), 0)
    strict = (iota((block, block), 0) < iota((block, block), 1)).astype(F32).astype(BF16)
    ones = jnp.ones((block, 128), BF16)
    pad[...] = jnp.zeros_like(pad)
    over = jnp.zeros((128, 128), F32)
    ranks = []
    for b in range(2):
        count = jnp.zeros((128, 128), F32)
        for q in range(NOB // block):
            own = owner_ref[b : b + 1, q * block : (q + 1) * block]
            hit = own == sub
            hit16 = hit.astype(F32).astype(BF16)
            before = dot_nn(hit16, strict) + jnp.concatenate([count] * (block // 128), axis=1)
            rank = jnp.sum(jnp.where(hit, before, 0.0), axis=0, keepdims=True).astype(jnp.int32)
            key_ref[b : b + 1, q * block : (q + 1) * block] = own * SLOTS + rank
            ranks.append(rank)
            count = count + dot_nn(hit16, ones)
        limit = jnp.full((128, 128), float(SLOTS), F32)
        if b == 0:
            limit = jnp.where(sub128 >= SLABS - 3, float(FAR_SLOTS), limit)
        over = jnp.maximum(over, jnp.where(count > limit, 1.0, 0.0))
    flag_ref[0, 0] = jnp.max(over).astype(jnp.int32)

    index0.wait()
    index1.wait()
    load.wait()
    slab = pltpu.make_async_copy(
        row.reshape(SLABS, TILES, 128), out_ref.at[:, 0:TILES, :], sems.at[2]
    )
    slab.start()

    for b, tile_s in enumerate((tile_s0, tile_s1)):

        def pick(i, carry, b=b, tile_s=tile_s):
            base = pl.multiple_of(i * unroll, unroll)
            for j in range(unroll):
                buf[pl.ds(b * NOB + base + j, 1), :] = row[pl.ds(tile_s[base + j], 1), :]
            return carry

        lax.fori_loop(0, NOB // unroll, pick, 0)

    for b in range(2):
        table = jnp.zeros((128, 128), F32)
        for q in range(NOB // block):
            own = owner_ref[b : b + 1, q * block : (q + 1) * block]
            hit = own == sub
            slot16 = (ranks[b * (NOB // block) + q] == (sub & (SLOTS - 1))).astype(F32).astype(BF16)
            pieces = []
            for k in range(block // 128):
                at = q * block + k * 128
                part = buf[b * NOB + at : b * NOB + at + 128, :].T
                lane = local_ref[b : b + 1, at : at + 128] & lane_bits
                pieces.append(jnp.sum(jnp.where(lane == sub128, part, 0.0), axis=0, keepdims=True))
            picked = jnp.concatenate(pieces, axis=1)
            three = dot_nt(jnp.concatenate(split3(jnp.where(hit, picked, 0.0)), axis=0), slot16)
            table = table + (three[0:128] + three[128:256] + three[256:384])
        pad[b, 8:136, :] = table

    low = iota((128, 128), 1) < SLOTS
    for r in range(4):
        pay[r] = jnp.where(
            low, pad[0, 4 + 2 * r : 132 + 2 * r, :], pad[0, 5 + 2 * r : 133 + 2 * r, :]
        )
    pay[4] = jnp.where(low, pad[0, 12:140, :], pad[1, 6:134, :])
    for r in range(2):
        pay[5 + r] = jnp.where(
            low, pad[1, 7 + 2 * r : 135 + 2 * r, :], pad[1, 8 + 2 * r : 136 + 2 * r, :]
        )
    lanes = iota((1, 128), 1)
    far = jnp.where(
        lanes < 32,
        pad[0, 133:134, :],
        jnp.where(
            lanes < 64,
            pltpu.roll(pad[0, 134:135, :], 32, 1),
            jnp.where(lanes < 96, pad[0, 135:136, :], pltpu.roll(pad[1, 135:136, :], 32, 1)),
        ),
    )
    pay[7] = jnp.broadcast_to(far, (128, 128))
    rows = [
        pltpu.make_async_copy(pay.at[r], out_ref.at[:, TILES + r, :], sems.at[5 + r])
        for r in range(8)
    ]
    for copy in rows:
        copy.start()
    slab.wait()
    for copy in rows:
        copy.wait()


def send(ensemble, obs_owner, obs_local):
    vmem = pl.BlockSpec(memory_space=pltpu.VMEM)
    smem = pl.BlockSpec(memory_space=pltpu.SMEM)
    hbm = pl.BlockSpec(memory_space=pl.ANY)
    return pl.pallas_call(
        send_kernel,
        out_shape=(
            jax.ShapeDtypeStruct((SLABS, ROWS_OUT, 128), F32),
            jax.ShapeDtypeStruct((2, NOB), jnp.int32),
            jax.ShapeDtypeStruct((1, 1), jnp.int32),
        ),
        in_specs=[hbm, vmem, vmem],
        out_specs=(hbm, vmem, smem),
        scratch_shapes=[
            pltpu.VMEM((VAR_DEV, 128), F32),
            pltpu.VMEM((2 * NOB, 128), F32),
            pltpu.VMEM((2, 144, 128), F32),
            pltpu.VMEM((8, SLABS, 128), F32),
            pltpu.VMEM((2, NOB), jnp.int32),
            pltpu.SMEM((NOB,), jnp.int32),
            pltpu.SMEM((NOB,), jnp.int32),
            pltpu.SemaphoreType.DMA((13,)),
        ],
        compiler_params=pltpu.CompilerParams(vmem_limit_bytes=60 << 20),
        cost_estimate=pl.CostEstimate(flops=10**9, bytes_accessed=5 << 20, transcendentals=0),
        name="send",
    )(ensemble.reshape(VAR_DEV, 128), obs_owner, obs_local)


SLOTS0 = 768
SLOTS1 = 512
CROSS_TILES = 256


def expansion(place, first):
    rank = iota((PER_TILE, place.shape[1]), 0).astype(F32) + first
    rows = [(place[t : t + 1, :] == rank).astype(F32).astype(BF16) for t in range(TILES)]
    return jnp.concatenate(rows, axis=0)


def expanded_weights(place, weights, first):
    rank = iota((PER_TILE, place.shape[1]), 0).astype(F32) + first
    picked = [
        jnp.where(place[t : t + 1, :] == rank, weights[t : t + 1, :], 0.0) for t in range(TILES)
    ]
    ones = jnp.ones((128, place.shape[1]), BF16)
    return sum(dot_nt(part, ones) for part in split3(jnp.concatenate(picked, axis=0)))


def tables_kernel(
    me_s,
    table_s,
    key_ref,
    owner_ref,
    local_ref,
    value_ref,
    errvar_ref,
    list_ref,
    index_ref,
    cross_ref,
    rounds_ref,
    *obs_refs,
):
    me = me_s[0, 0]
    at_far = me == FAR_SLAB
    near_far = (me >= FAR_SLAB - 2) & (me <= FAR_SLAB + 2)

    def slot_key(slab, rank, keep):
        return jnp.where(keep & (slab >= 0) & (slab < SLABS), slab * SLOTS + rank, -1)

    j = iota((SLOTS0, 128), 0)
    f = j - 640
    near = slot_key(me - 4 + lax.shift_right_logical(j, 6), j & 63, j < 576)
    far = slot_key(SLABS - 3 + lax.shift_right_arithmetic(f, 5), f & 31, (f < 96) & near_far)
    keys0 = jnp.where(j < 640, near, far)
    j = iota((SLOTS1, 128), 0)
    f = j - 384
    near = slot_key(me - 3 + lax.shift_right_logical(j, 6), j & 63, j >= 64)
    far = slot_key(jnp.full_like(j, SLABS - 1), f - 96, (f >= 96) & at_far)
    keys1 = jnp.where(j < 384, near, far)

    def tile_id(shape):
        k = iota(shape, 0)
        near_id = (me - 2) * TILES + k
        far_id = jnp.where((k < 192) & at_far, (SLABS - 1) * TILES + k - 160, -2)
        return jnp.where(k < 160, jnp.where(near_id < 0, -2, near_id), far_id)

    def on_tiles(b, ids):
        total = jnp.zeros(ids.shape, F32)
        for k in range(8):
            entry = index_ref[b, k : k + 1, :]
            pick = jnp.zeros(entry.shape, F32)
            for n in range(16):
                pick = jnp.where(entry == n, table_s[n], pick)
            total = total + jnp.where(list_ref[b, k : k + 1, :] == ids, pick, 0.0)
        return total

    def exact_nt(a, b):
        return sum(dot_nt(part, b) for part in split3(a))

    ids = tile_id((CROSS_TILES, NOB))
    own_ids = me * TILES + iota((TILES, NOB), 0)
    for b, keys in enumerate((keys0, keys1)):
        lines_ref, w_ref, place_ref, wide_ref = obs_refs[4 * b : 4 * b + 4]
        slots = keys.shape[0]
        select = jnp.concatenate(
            [
                (keys == key_ref[b : b + 1, c * 128 : (c + 1) * 128]).astype(F32).astype(BF16)
                for c in range(NOB // 128)
            ],
            axis=1,
        )
        own_tile = owner_ref[b : b + 1, :] * TILES + lax.shift_right_logical(local_ref[b : b + 1, :], 7)
        lines = jnp.concatenate(
            [
                value_ref[b : b + 1, :],
                errvar_ref[b : b + 1, :] - 1.0,
                own_tile.astype(F32) + 1.0,
                jnp.zeros((5, NOB), F32),
            ],
            axis=0,
        )
        lines = exact_nt(lines, select)
        weights = exact_nt(on_tiles(b, own_ids), select)
        hits = (weights != 0.0).astype(F32)
        upto = (iota((slots, slots), 0) <= iota((slots, slots), 1)).astype(F32).astype(BF16)
        upto_hits = dot_nn(hits.astype(BF16), upto)
        most = jnp.max(upto_hits).astype(jnp.int32)
        rounds_ref[b] = jnp.maximum((most + PER_TILE - 1) // PER_TILE, 1)
        place = jnp.where(weights != 0.0, upto_hits - 1.0, -1.0)
        place_ref[...] = place
        w_ref[...] = weights
        wide_ref[...] = expanded_weights(place, weights, 0)
        lines_ref[...] = jnp.concatenate(
            [lines[0:1, :], lines[1:2, :] + 1.0, jnp.zeros((6, slots), F32)], axis=0
        )
        if b == 0:
            spread = on_tiles(0, ids)
            spread = [dot_nt(select, part).astype(BF16) for part in split3(spread)]
        else:
            own_row = lines[2:3, :].astype(jnp.int32) - 1
            meet = (own_row == tile_id((CROSS_TILES, slots))).astype(F32).astype(BF16)
            cross_ref[...] = sum(dot_nn(part, meet) for part in spread)


def tables(me, key, obs_owner, obs_local, obs_value, obs_errvar, tile_list, weight_index, weight_table):
    vmem = pl.BlockSpec(memory_space=pltpu.VMEM)
    smem = pl.BlockSpec(memory_space=pltpu.SMEM)
    per_obs = [
        shape
        for slots in (SLOTS0, SLOTS1)
        for shape in (
            jax.ShapeDtypeStruct((8, slots), F32),
            jax.ShapeDtypeStruct((TILES, slots), F32),
            jax.ShapeDtypeStruct((TILES, slots), F32),
            jax.ShapeDtypeStruct((TILES * PER_TILE, 128), F32),
        )
    ]
    return pl.pallas_call(
        tables_kernel,
        out_shape=(
            jax.ShapeDtypeStruct((SLOTS0, SLOTS1), F32),
            jax.ShapeDtypeStruct((2,), jnp.int32),
            *per_obs,
        ),
        in_specs=[smem, smem] + [vmem] * 7,
        out_specs=(vmem, smem) + (vmem,) * 8,
        compiler_params=pltpu.CompilerParams(vmem_limit_bytes=60 << 20),
        cost_estimate=pl.CostEstimate(flops=10**6, bytes_accessed=10**6, transcendentals=0),
        name="tables",
    )(
        me.reshape(1, 1).astype(jnp.int32),
        weight_table,
        key,
        obs_owner,
        obs_local,
        obs_value,
        obs_errvar,
        jnp.transpose(tile_list, (0, 2, 1)),
        jnp.transpose(weight_index, (0, 2, 1)),
    )


def obs_stats(priors, lines):
    value, errvar = lines[0:1, :], lines[1:2, :]
    mean = jnp.mean(priors, axis=0, keepdims=True)
    dev = priors - mean
    spread = jnp.sum(dev * dev, axis=0, keepdims=True) / (MEMBERS - 1.0)
    denominator = spread + errvar
    post_mean = (errvar * mean + spread * value) / denominator
    shift = post_mean - mean + (jnp.sqrt(errvar / denominator) - 1.0) * dev
    scale = 1.0 / ((MEMBERS - 1.0) * (spread + epsilon))
    return dev, shift * scale


def analyse_kernel(rounds_s, r_ref, cross_ref, *refs):
    obs_refs, (out_ref, x_ref, total_ref, sems, pay, slab, cross, *more) = refs[:8], refs[8:]
    expand, wide = more[:2], more[2:]
    sources = [r_ref.at[:, TILES:ROWS_OUT, :], cross_ref]
    sources += [obs_refs[3], obs_refs[7], r_ref.at[:, 0:TILES, :]]
    arrive = [
        pltpu.make_async_copy(source, place, sems.at[TILES + k])
        for k, (source, place) in enumerate(zip(sources, [pay, cross, *wide, slab]))
    ]
    for copy in arrive:
        copy.start()

    def tile(t):
        return slab.reshape(MEMBERS * TILES, 128)[pl.ds(t, MEMBERS, stride=TILES), :]

    for b in range(2):
        expand[b][...] = expansion(obs_refs[4 * b + 2][...], 0)
    arrive[0].wait()
    part_rows = [pay.reshape(MEMBERS * 8, 128)[pl.ds(r, MEMBERS, stride=8), :] for r in range(8)]
    priors0 = jnp.concatenate([part_rows[r] for r in (0, 1, 2, 3, 4, 7)], axis=1)
    priors1 = jnp.concatenate([part_rows[r] for r in (4, 5, 6, 7)], axis=1)
    dev0, gain0 = obs_stats(priors0, obs_refs[0])
    dev_hi, dev_lo = split2(dev0)
    z_dev = priors1 - jnp.mean(priors1, axis=0, keepdims=True)
    z_hi, z_lo = split2(z_dev)
    covariance = dot_tn(
        jnp.concatenate([dev_hi, dev_lo], axis=0), jnp.concatenate([z_hi, z_hi], axis=0)
    ) + dot_tn(dev_hi, z_lo)
    arrive[1].wait()
    c_hi, c_lo = split2(covariance * cross[...])
    g_hi, g_lo = split2(gain0)
    priors1 = priors1 + (dot_nn(g_hi, c_hi) + dot_nn(g_lo, c_hi) + dot_nn(g_hi, c_lo))
    dev1, gain1 = obs_stats(priors1, obs_refs[4])
    dev_parts = [jnp.concatenate(split2(dev), axis=0) for dev in (dev0, dev1)]
    gain_parts = [jnp.concatenate(split2(gain), axis=0) for gain in (gain0, gain1)]

    def per_hit(b, expand, wide):
        dev = dot_nt(expand, dev_parts[b]).astype(BF16)
        gain = dot_nt(expand, gain_parts[b])
        first, second = split2((gain[:, :128] + gain[:, 128:]) * wide)
        return dev[:, :128], dev[:, 128:], first, second

    def increments_of(pair, hits, xs):
        lhs, rhs = [], []
        for k, t in enumerate(pair):
            dev_hi, dev_lo, gain_hi, gain_lo = [h[PER_TILE * t : PER_TILE * (t + 1)] for h in hits]
            x = xs[k]
            hi, lo = split2(x - jnp.mean(x, axis=0, keepdims=True))
            four = dot_nn(jnp.concatenate([dev_hi, dev_lo], axis=0), jnp.concatenate([hi, lo], axis=1))
            four = four[:PER_TILE] + four[PER_TILE:]
            c_hi, c_lo = split2(four[:, :128] + four[:, 128:])
            zero = jnp.zeros((3 * PER_TILE, 128), BF16)
            block = jnp.concatenate([c_hi, c_hi, c_lo], axis=0)
            rhs.append(jnp.concatenate([block, zero] if k == 0 else [zero, block], axis=1))
            lhs.extend([gain_hi, gain_lo, gain_hi])
        step = dot_tn(jnp.concatenate(lhs, axis=0), jnp.concatenate(rhs, axis=0))
        return [step[:, :128], step[:, 128:]]

    def send_home(tiles):
        copies = []
        for t in tiles:
            copy = pltpu.make_async_copy(x_ref.at[t], out_ref.at[:, t, :], sems.at[t])
            copy.start()
            copies.append(copy)
        return copies

    for copy in arrive[2:]:
        copy.wait()
    one_round = (rounds_s[0] <= 1) & (rounds_s[1] <= 1)

    @pl.when(one_round)
    def _():
        hits = [per_hit(b, expand[b][...], wide[b][...]) for b in range(2)]
        leave = []
        for start in range(0, TILES, GROUP):
            xs = [tile(t) for t in range(start, start + GROUP)]
            for b in range(2):
                steps = []
                for k in range(0, GROUP, 2):
                    steps.extend(increments_of((start + k, start + k + 1), hits[b], xs[k : k + 2]))
                xs = [x + step for x, step in zip(xs, steps)]
            for k in range(GROUP):
                x_ref[start + k] = xs[k]
            leave.extend(send_home(range(start, start + GROUP)))
        for copy in leave:
            copy.wait()

    @pl.when(jnp.logical_not(one_round))
    def _():
        for t in range(TILES):
            x_ref[t] = tile(t)
        for b in range(2):
            total_ref[...] = jnp.zeros_like(total_ref)

            def one(r, carry, b=b):
                first = (r * PER_TILE).astype(F32)
                place, weights = obs_refs[4 * b + 2][...], obs_refs[4 * b + 1][...]
                hits = per_hit(b, expansion(place, first), expanded_weights(place, weights, first))
                for t in range(0, TILES, 2):
                    steps = increments_of((t, t + 1), hits, [x_ref[t], x_ref[t + 1]])
                    total_ref[t] = total_ref[t] + steps[0]
                    total_ref[t + 1] = total_ref[t + 1] + steps[1]
                return carry

            lax.fori_loop(0, rounds_s[b], one, 0)
            x_ref[...] = x_ref[...] + total_ref[...]
        for copy in send_home(range(TILES)):
            copy.wait()


def analyse_slab(received, cross, rounds, *obs):
    vmem = pl.BlockSpec(memory_space=pltpu.VMEM)
    smem = pl.BlockSpec(memory_space=pltpu.SMEM)
    hbm = pl.BlockSpec(memory_space=pl.ANY)
    return pl.pallas_call(
        analyse_kernel,
        out_shape=jax.ShapeDtypeStruct((MEMBERS, TILES, 128), F32),
        in_specs=[smem, hbm, hbm] + [vmem, vmem, vmem, hbm] * 2,
        out_specs=hbm,
        scratch_shapes=[
            pltpu.VMEM((TILES, MEMBERS, 128), F32),
            pltpu.VMEM((TILES, MEMBERS, 128), F32),
            pltpu.SemaphoreType.DMA((TILES + 5,)),
            pltpu.VMEM((MEMBERS, 8, 128), F32),
            pltpu.VMEM((MEMBERS, TILES, 128), F32),
            pltpu.VMEM((SLOTS0, SLOTS1), F32),
            pltpu.VMEM((TILES * PER_TILE, SLOTS0), BF16),
            pltpu.VMEM((TILES * PER_TILE, SLOTS1), BF16),
            pltpu.VMEM((TILES * PER_TILE, 128), F32),
            pltpu.VMEM((TILES * PER_TILE, 128), F32),
        ],
        compiler_params=pltpu.CompilerParams(vmem_limit_bytes=60 << 20),
        cost_estimate=pl.CostEstimate(flops=4 * 10**9, bytes_accessed=8 << 20, transcendentals=0),
        name="analyse",
    )(rounds, received, cross, *obs)


def body(
    ensemble, obs_owner, obs_local, obs_value, obs_errvar, tile_list, weight_index, weight_table
):
    me = lax.axis_index("gx") * lax.axis_size("gy") + lax.axis_index("gy")
    obs = (obs_owner, obs_local, obs_value, obs_errvar, tile_list, weight_index, weight_table)
    outgoing, key, flag = send(ensemble, obs_owner, obs_local)

    received = lax.all_to_all(outgoing, AXES, split_axis=0, concat_axis=0, tiled=True)
    updated = analyse_slab(received, *tables(me, key, *obs))

    def overflows(state):
        return state[0] > 0

    def redo(state):
        slabs = received[:, :TILES, :].reshape(MEMBERS, VAR_DEV)
        return jnp.int32(0), general(slabs, me, *obs).reshape(MEMBERS, TILES, 128)

    updated = lax.while_loop(overflows, redo, (flag[0, 0], updated))[1]
    result = lax.all_to_all(updated, AXES, split_axis=0, concat_axis=0, tiled=True)
    return result.reshape(ensemble.shape)


def solution(mesh):
    placed = (P(("gx", "gy"), None), P(), P(), P(), P(), P(), P(), P())
    return jax.shard_map(
        body, mesh=mesh, in_specs=placed, out_specs=P(("gx", "gy"), None), check_vma=False
    )
```
